32 devices in a mesh: shell: 1, row: 4 (over z), col: 8 (over y, x, core).
Axes of the slice: x: 2, y: 2, z: 4, core: 2. Of those that a mesh axis runs over, the one named last changes fastest.
Arguments:
- convergence: bfloat16 [1, 16384, 16384], P('shell', ('row', 'col')), may hold values from -6 to 6
- lens_weight: float32 [1], P('shell'), may hold values from 0.3 to 1
- rays_in: float32 [6, 1024, 16384], P(None, ('row', 'col')), may hold values from -6 to 6
Outputs:
- rays_out: float32 [1, 6, 1024, 16384], P('shell', None, ('row', 'col'))
The draws below stay inside these ranges and needn't reach their ends.
All inputs are finite; a program needn't handle non-finite values.
Results may differ from the reference program's by a relative error of at most 0.0003.
Values sent between devices are 32-bit elements; how exact they have to be, the bound alone decides.
No kernel may reach another device: no remote copies, remote signals or barrier semaphores. Data moves between devices by JAX's collectives and lax.ppermute only.
A program may use at most 256 MiB of HBM per device.

```python
import math
import jax
import jax.numpy as jnp
from jax import lax

GRID = 16384
STRIDE = 16
SHELLS = 1
RAYS = 1024


def block_scale(stream_key, shape, pieces, least, top_value):
    gain, own = 1.0, jax.random.fold_in(stream_key, 6)
    for position, blocks in pieces:
        steps = jnp.exp(jax.random.uniform(jax.random.fold_in(own, position), (blocks,), jnp.float32, least / len(pieces), top_value / len(pieces)))
        gain = gain * jnp.repeat(steps, shape[position] // blocks).reshape([-1 if axis == position else 1 for axis in range(len(shape))])
    return gain


def gaussian(rng, shape, scale, limit, pieces=(), held_as=jnp.bfloat16):
    loudness = block_scale(rng, shape, pieces, -0.22, 0.18) if pieces else 1.0
    drawn = jax.random.normal(rng, shape, jnp.float32) * scale * loudness
    return jnp.minimum(jnp.maximum(drawn, -limit), limit).astype(held_as)


def setup_inputs(seed: int = 0) -> dict:
    arg_keys = jax.random.split(jax.random.key(seed), 4)
    convergence = gaussian(arg_keys[0], (SHELLS, GRID, GRID), 1.0, 6.0, ((1, 32),))
    lens_weight = jnp.clip(jax.random.uniform(arg_keys[1], (SHELLS,), jnp.float32, 0.3, 1.0), 0.3, 1.0)
    rays_in = gaussian(arg_keys[2], (6, RAYS, GRID), 1.0, 6.0, ((1, 32),), jnp.float32)
    return dict(convergence=convergence, lens_weight=lens_weight, rays_in=rays_in)


def shell_fields(kappa):
    length = kappa.shape[0]
    half = length // 2
    span = length // STRIDE
    spectrum = jnp.fft.rfft2(kappa.astype(jnp.float32))[:, :half]
    wave_cols = (2.0 * math.pi / length) * jnp.arange(half).astype(jnp.float32)

    def accumulate(total, alias):
        frequency = alias * span + jnp.arange(span, dtype=jnp.int32)
        signed = jnp.where(frequency < half, frequency, frequency - length).astype(jnp.float32)
        wave_rows = (2.0 * math.pi / length) * signed
        rows_part = wave_rows[:, None]
        cols_part = wave_cols[None, :]
        squared = rows_part * rows_part + cols_part * cols_part
        valid = (squared > 0.0) & (frequency != half)[:, None]
        scale = jnp.where(valid, -2.0 / jnp.where(valid, squared, 1.0), 0.0)
        piece = lax.dynamic_slice_in_dim(spectrum, alias * span, span, 0) * scale
        terms = jnp.stack([1j * rows_part * piece, 1j * cols_part * piece, -rows_part * rows_part * piece,
                           -cols_part * cols_part * piece, -rows_part * cols_part * piece])
        return total + terms, None

    total, _ = lax.scan(accumulate, jnp.zeros((5, span, half), spectrum.dtype), jnp.arange(STRIDE, dtype=jnp.int32))
    rows_done = jnp.fft.ifft(total, axis=1) / STRIDE
    return jnp.fft.irfft(rows_done, n=length, axis=2)


def advance(state, fields, weight):
    shift_rows = state[0] - weight * fields[0]
    shift_cols = state[1] - weight * fields[1]
    curve_rows, curve_cols, curve_mixed = fields[2], fields[3], fields[4]
    upper_left, upper_right, lower_left, lower_right = state[2], state[3], state[4], state[5]
    new_ul = upper_left - weight * (curve_rows * upper_left + curve_mixed * lower_left)
    new_ur = upper_right - weight * (curve_rows * upper_right + curve_mixed * lower_right)
    new_ll = lower_left - weight * (curve_mixed * upper_left + curve_cols * lower_left)
    new_lr = lower_right - weight * (curve_mixed * upper_right + curve_cols * lower_right)
    return jnp.stack([shift_rows, shift_cols, new_ul, new_ur, new_ll, new_lr])


def reference(convergence, lens_weight, rays_in):
    state = rays_in
    results = []
    for shell in range(SHELLS):
        fields = shell_fields(convergence[shell])
        state = advance(state, fields, lens_weight[shell])
        results.append(state)
    return jnp.stack(results)
```

```python
import functools
import math

import jax
import jax.numpy as jnp
import numpy as np
from jax import lax
from jax.experimental import pallas as pl
from jax.experimental.pallas import tpu as pltpu
from jax.sharding import PartitionSpec as P

STRIDE = 16
LANES = 128
TILE = 8
VMEM = 56 * 2**20
F32 = jnp.float32
BF16 = jnp.bfloat16


def plus(a, b):
    return b if a is None else a if b is None else a + b


def minus(a, b):
    return a if b is None else -b if a is None else a - b


def turned(value, numerator, denominator):
    numerator %= denominator
    real, imaginary = value
    eighth = 8 * numerator / denominator
    if eighth == 0:
        return value
    if eighth == 2:
        return (None if imaginary is None else -imaginary, real)
    if eighth == 4:
        return (-real, None if imaginary is None else -imaginary)
    if eighth == 6:
        return (imaginary, None if real is None else -real)
    cosine = math.cos(2 * math.pi * numerator / denominator)
    sine = math.sin(2 * math.pi * numerator / denominator)
    if real is None:
        return (imaginary * -sine, imaginary * cosine)
    if imaginary is None:
        return (real * cosine, real * sine)
    if eighth in (1, 3, 5, 7):
        scale = math.sqrt(0.5)
        if eighth == 1:
            return ((real - imaginary) * scale, (real + imaginary) * scale)
        if eighth == 3:
            return ((real + imaginary) * -scale, (real - imaginary) * scale)
        if eighth == 5:
            return ((imaginary - real) * scale, (real + imaginary) * -scale)
        return ((real + imaginary) * scale, (imaginary - real) * scale)
    return (real * cosine - imaginary * sine, real * sine + imaginary * cosine)


def c_add(a, b):
    return (plus(a[0], b[0]), plus(a[1], b[1]))


def c_sub(a, b):
    return (minus(a[0], b[0]), minus(a[1], b[1]))


def conj(a):
    return (a[0], None if a[1] is None else -a[1])


def fft_complex(values):
    count = len(values)
    if count == 1:
        return list(values)
    even, odd = fft_complex(values[0::2]), fft_complex(values[1::2])
    out = [None] * count
    for k in range(count // 2):
        term = turned(odd[k], -k, count)
        out[k] = c_add(even[k], term)
        out[k + count // 2] = c_sub(even[k], term)
    return out


def fft_real(values):
    count = len(values)
    if count == 1:
        return [(values[0], None)]
    if count == 2:
        return [(values[0] + values[1], None), (values[0] - values[1], None)]
    even, odd = fft_real(values[0::2]), fft_real(values[1::2])
    out = [None] * (count // 2 + 1)
    for k in range(count // 4 + 1):
        term = turned(odd[k], -k, count)
        out[k] = c_add(even[k], term)
        if k < count // 4:
            low = c_sub(even[k], term)
            real, imaginary = low
            if imaginary is not None:
                imaginary = term[1] - even[k][1] if even[k][1] is not None else term[1]
            out[count // 2 - k] = (real, imaginary)
    return out


def ifft_real(values, count):
    if count == 2:
        return [values[0][0] + values[1][0], values[0][0] - values[1][0]]
    even, odd = [], []
    for k in range(count // 4 + 1):
        a, b = values[k], values[count // 2 - k]
        if k == count // 4:
            even.append((a[0] + a[0], None))
            odd.append((-(a[1] + a[1]), None))
        elif k == 0:
            even.append((a[0] + b[0], None))
            odd.append((a[0] - b[0], None))
        else:
            even.append((a[0] + b[0], a[1] - b[1]))
            odd.append(turned((a[0] - b[0], a[1] + b[1]), k, count))
    out = [None] * count
    out[0::2] = ifft_real(even, count // 2)
    out[1::2] = ifft_real(odd, count // 2)
    return out


def halves(table):
    table = np.asarray(table, np.float32)
    high = table.astype(jnp.bfloat16)
    low = (table - high.astype(np.float32)).astype(jnp.bfloat16)
    return high, low


def column_bins(length):
    groups = length // LANES
    slot = np.arange(groups // 2)[:, None]
    lane = np.arange(LANES)[None, :]
    bins = slot + groups * lane
    bins = np.where(bins >= length // 2, bins - length, bins)
    half = LANES // 2
    bins[0] = np.where(lane[0] < half, groups * lane[0], groups // 2 + groups * (lane[0] - half))
    return bins


def column_table(length):
    bins = column_bins(length)
    slots = bins.shape[0]
    angle = 2 * np.pi / length * (bins[:, None, :] * np.arange(LANES)[None, :, None] % length)
    cosine, sine = np.cos(angle), np.sin(angle)
    table = np.zeros((slots, 2 * LANES, 2 * LANES))
    table[:, :LANES, :LANES] = cosine
    table[:, :LANES, LANES:] = -sine
    table[:, LANES:, :LANES] = sine
    table[:, LANES:, LANES:] = cosine
    half = LANES // 2
    first = np.zeros((2 * LANES, 2 * LANES))
    for begin, rows in ((0, slice(0, LANES)), (half, slice(LANES, 2 * LANES))):
        lanes = slice(begin, begin + half)
        first[rows, begin : begin + half] = cosine[0][:, lanes]
        first[rows, LANES + begin : LANES + begin + half] = -sine[0][:, lanes]
    table[0] = first
    high, low = halves(table)
    return np.concatenate([high, low], axis=1)


def ray_tables(rays, plane_rays, length):
    pairs = rays // 2
    rows = pairs + TILE
    order = np.arange(rows)
    angle = 2 * np.pi / rays * (order[:, None] * np.arange(plane_rays)[None, :] % rays)
    keep = (order <= pairs)[:, None]
    forward = np.concatenate([np.where(keep, np.cos(angle), 0), np.where(keep, -np.sin(angle), 0)])
    high, low = halves(forward)
    forward = np.concatenate([high, low, high], axis=1)
    turn = 2 * np.pi / length * (order[:, None] * np.arange(STRIDE)[None, :] % length)
    twist = np.zeros((rows, LANES), np.float32)
    twist[:, :STRIDE] = np.cos(turn)
    twist[:, STRIDE : 2 * STRIDE] = -np.sin(turn)
    angle = 2 * np.pi / rays * (np.arange(rays)[:, None] * np.arange(pairs)[None, :] % rays)
    cosine = np.cos(angle)
    cosine[:, 0] = 0.5
    backward = np.concatenate([cosine, np.sin(angle)], axis=1)
    high, low = halves(backward)
    return forward, twist, np.concatenate([high, low], axis=1)


def split(value):
    high = value.astype(BF16)
    return high, (value - high.astype(F32)).astype(BF16)


def dot(left, right):
    return jnp.dot(left, right, preferred_element_type=F32)


def params():
    return pltpu.CompilerParams(vmem_limit_bytes=VMEM)


def groups_kernel(x_ref, y_ref, sum_ref):
    rows, length = x_ref.shape
    groups = length // LANES

    @pl.when(pl.program_id(0) == 0)
    def _():
        sum_ref[...] = jnp.zeros_like(sum_ref)

    def step(index, carry):
        first = pl.multiple_of(index * 2 * TILE, 2 * TILE)
        for half in range(2):
            blocks = []
            for u in range(groups):
                lanes = slice(u * LANES, (u + 1) * LANES)
                block = x_ref[pl.ds(first, 2 * TILE), lanes].astype(F32)
                block = block[half * TILE : (half + 1) * TILE]
                sum_ref[:, lanes] += block
                blocks.append(block)
            bins = fft_real(blocks)
            place = pl.ds(pl.multiple_of(first + half * TILE, TILE), TILE)
            for slot in range(groups // 2):
                real, imaginary = bins[slot]
                if slot == 0:
                    imaginary = bins[groups // 2][0]
                y_ref[slot, 0, place] = real
                y_ref[slot, 1, place] = imaginary
        return carry

    lax.fori_loop(0, rows // (2 * TILE), step, 0)


def over_groups(field):
    rows, length = field.shape
    slots = length // LANES // 2
    step = min(rows, 32)
    return pl.pallas_call(
        groups_kernel,
        grid=(rows // step,),
        in_specs=[pl.BlockSpec((step, length), lambda i: (i, 0))],
        out_specs=[
            pl.BlockSpec((slots, 2, step, LANES), lambda i: (0, 0, i, 0)),
            pl.BlockSpec((TILE, length), lambda i: (0, 0)),
        ],
        out_shape=[
            jax.ShapeDtypeStruct((slots, 2, rows, LANES), F32),
            jax.ShapeDtypeStruct((TILE, length), F32),
        ],
        compiler_params=params(),
        cost_estimate=pl.CostEstimate(
            flops=20 * rows * length, bytes_accessed=6 * rows * length, transcendentals=0
        ),
        name="column_groups",
    )(field)


def lanes_kernel(y_ref, table_ref, out_ref):
    own = y_ref.shape[2] // STRIDE
    sides = []
    for side in range(2):
        pieces = [y_ref[0, side, pl.ds(s, own, stride=STRIDE), :] for s in range(STRIDE)]
        whole = jnp.concatenate(pieces, axis=0)
        sides.append(whole)
    high, low = split(jnp.concatenate(sides, axis=1))
    table = table_ref[0]
    top, rest = table[: 2 * LANES], table[2 * LANES :]
    out_ref[0, 0] = dot(
        jnp.concatenate([high, high, low], axis=1), jnp.concatenate([top, rest, top], axis=0)
    )


def over_lanes(grouped, table, devices, begin, count):
    slots, _, rows, lanes = grouped.shape
    width = 2 * lanes
    owned = slots // devices
    return pl.pallas_call(
        lanes_kernel,
        grid=(devices, count),
        in_specs=[
            pl.BlockSpec(
                (1, 2, rows, lanes), lambda d, i: (d * owned + begin + i, 0, 0, 0)
            ),
            pl.BlockSpec((1, 2 * width, width), lambda d, i: (d * owned + begin + i, 0, 0)),
        ],
        out_specs=pl.BlockSpec((1, 1, rows, width), lambda d, i: (d, i, 0, 0)),
        out_shape=jax.ShapeDtypeStruct((devices, count, rows, width), F32),
        compiler_params=params(),
        cost_estimate=pl.CostEstimate(
            flops=6 * devices * count * rows * width * width,
            bytes_accessed=8 * devices * count * rows * width,
            transcendentals=0,
        ),
        name="column_lanes",
    )(grouped, table)


def rays_kernel(has_mean, place_ref, mean_ref, x_ref, forward_ref, twist_ref, backward_ref, out_ref, cos_ref, sin_ref,
                pq_ref, ab_ref, high_ref, low_ref):
    sources, _, _, own, width = x_ref.shape
    planes = out_ref.shape[0]
    plane_rays = sources * own
    rays = planes * plane_rays
    pairs = rays // 2
    rows = pairs + TILE
    length = rays * STRIDE
    half = length // 2
    groups = length // LANES

    @pl.when(pl.program_id(0) == 0)
    def _():
        for s in range(STRIDE):
            cos_ref[s] = jnp.broadcast_to(twist_ref[:, s : s + 1], (rows, LANES))
            sin_ref[s] = jnp.broadcast_to(
                twist_ref[:, STRIDE + s : STRIDE + s + 1], (rows, LANES)
            )

    if has_mean:
        at_mean = lax.broadcasted_iota(jnp.int32, (1, width), 1) == 0
        at_mean = jnp.logical_and(at_mean, place_ref[1] + pl.program_id(0) == 0)
        offset = jnp.where(at_mean, mean_ref[0] * float(length), 0.0)

    def forward(s, carry):
        value = x_ref[:, 0, s].reshape(plane_rays, width)
        if has_mean:
            value = value - offset
        high, low = split(value)
        pq_ref[s] = dot(forward_ref[...], jnp.concatenate([high, high, low], axis=0))
        return carry

    lax.fori_loop(0, STRIDE, forward, 0)

    slot = place_ref[1] + pl.program_id(0)
    lane = lax.broadcasted_iota(jnp.int32, (TILE, LANES), 1)
    bins = slot + groups * lane
    bins = jnp.where(bins >= half, bins - length, bins)
    middle = LANES // 2
    first = jnp.where(lane < middle, groups * lane, groups // 2 + groups * (lane - middle))
    bins = jnp.where(slot == 0, first, bins).astype(F32)
    bins_squared = bins * bins
    sublane = lax.broadcasted_iota(jnp.int32, (TILE, LANES), 0)

    def filtered(block, carry):
        base = pl.multiple_of(block * TILE, TILE)
        at_p = pl.ds(base, TILE)
        at_q = pl.ds(pl.multiple_of(rows + base, TILE), TILE)
        order = (sublane + base).astype(F32)
        weights, wave_weights = [], []
        for a in range(STRIDE):
            wave = order + float(a * rays - (length if a >= STRIDE // 2 else 0))
            squared = wave * wave + bins_squared
            if a == 0:
                squared_safe = jnp.where(squared > 0.0, squared, 1.0)
            else:
                squared_safe = squared
            inverse = pl.reciprocal(squared_safe, approx=True)
            inverse = inverse * (2.0 - squared_safe * inverse)
            inverse = inverse * (2.0 - squared_safe * inverse)
            if a == 0:
                inverse = jnp.where(squared > 0.0, inverse, 0.0)
            if a == STRIDE // 2:
                inverse = jnp.where(order > 0.0, inverse, 0.0)
            weights.append(inverse)
            wave_weights.append(inverse * wave)
        sums = []
        for side in range(2):
            values = []
            for s in range(STRIDE):
                pr, pi = pq_ref[s, at_p, :LANES], pq_ref[s, at_p, LANES:]
                qr, qi = pq_ref[s, at_q, :LANES], pq_ref[s, at_q, LANES:]
                real, imaginary = (pr - qi, pi + qr) if side == 0 else (pr + qi, qr - pi)
                if s > 0:
                    cosine, sine = cos_ref[s, at_p], sin_ref[s, at_p]
                    real, imaginary = (
                        real * cosine - imaginary * sine,
                        real * sine + imaginary * cosine,
                    )
                values.append((real, imaginary))
            spectrum = fft_complex(values)
            for chosen in (weights, wave_weights):
                for which in range(2):
                    total = spectrum[0][which] * chosen[0]
                    for a in range(1, STRIDE):
                        total = total + spectrum[a][which] * chosen[a]
                    sums.append(total)
        a0r, a0i, a1r, a1i, b0r, b0i, b1r, b1i = sums
        even = (a0r + b0r, a0i - b0i, a1r - b1r, a1i + b1i)
        odd = (a0r - b0r, a0i + b0i, a1r + b1r, a1i - b1i)
        for index, value in enumerate(even):
            ab_ref[0, at_p, index * LANES : (index + 1) * LANES] = value
        for index, value in enumerate((-odd[1], odd[0], -odd[3], odd[2])):
            ab_ref[1, at_p, index * LANES : (index + 1) * LANES] = value
        return carry

    lax.fori_loop(0, rows // TILE, filtered, 0)

    for side in range(2):
        high, low = split(ab_ref[side, :pairs])
        high_ref[side * pairs : (side + 1) * pairs] = high
        low_ref[side * pairs : (side + 1) * pairs] = low
    last = ab_ref[0, pairs : pairs + TILE][:1] * 0.5
    parity = lax.broadcasted_iota(jnp.int32, (plane_rays, 4 * LANES), 0) % 2
    tail = jnp.where(parity == 0, last, -last)

    def backward(shift, carry):
        at = pl.ds(pl.multiple_of(shift * plane_rays, plane_rays), plane_rays)
        total = dot(backward_ref[at, :rays], high_ref[...])
        total += dot(backward_ref[at, rays:], high_ref[...])
        total += dot(backward_ref[at, :rays], low_ref[...])
        plane = lax.rem(place_ref[0] + shift, planes)
        out_ref[plane, :, 0] = (total + tail).reshape(sources, own, 4 * LANES)
        return carry

    lax.fori_loop(0, planes, backward, 0)


def to_rays(place, mean, arrived, tables, planes):
    sources, count, strides, own, width = arrived.shape
    forward, twist, backward = tables
    rays = planes * sources * own
    rows = rays // 2 + TILE

    def whole(array):
        return pl.BlockSpec(
            array.shape, lambda i, place: (0, 0), pipeline_mode=pl.Buffered(1)
        )

    return pl.pallas_call(
        functools.partial(rays_kernel, mean is not None),
        grid_spec=pltpu.PrefetchScalarGridSpec(
            num_scalar_prefetch=1,
            grid=(count,),
            in_specs=[
                pl.BlockSpec(memory_space=pltpu.SMEM),
                pl.BlockSpec(
                    (sources, 1, strides, own, width), lambda i, place: (0, i, 0, 0, 0)
                ),
                whole(forward),
                whole(twist),
                whole(backward),
            ],
            out_specs=pl.BlockSpec(
                (planes, sources, 1, own, 4 * LANES), lambda i, place: (0, 0, i, 0, 0)
            ),
            scratch_shapes=[
                pltpu.VMEM((STRIDE, rows, LANES), F32),
                pltpu.VMEM((STRIDE, rows, LANES), F32),
                pltpu.VMEM((STRIDE, 2 * rows, width), F32),
                pltpu.VMEM((2, rows, 4 * LANES), F32),
                pltpu.VMEM((rays, 4 * LANES), BF16),
                pltpu.VMEM((rays, 4 * LANES), BF16),
            ],
        ),
        out_shape=jax.ShapeDtypeStruct((planes, sources, count, own, 4 * LANES), F32),
        compiler_params=params(),
        cost_estimate=pl.CostEstimate(
            flops=8 * count * (6 * STRIDE * 2 * rows * sources * own * width
                           + 6 * rays * rays * 4 * LANES),
            bytes_accessed=4 * arrived.size + 16 * count * rays * LANES,
            transcendentals=0,
        ),
        name="ray_rows",
    )(place, jnp.zeros(1, F32) if mean is None else mean, arrived, forward, twist, backward)


def back_kernel(t_ref, table_ref, factor_ref, out_ref):
    t = t_ref[0, 0]
    t0r, t0i, t1r, t1i = (t[:, n * LANES : (n + 1) * LANES] for n in range(4))
    factor = factor_ref[0]
    by_r, by_c, by_cc, by_rc = (factor[n : n + 1] for n in range(4))
    real = jnp.concatenate([-t1i * by_r, -t0i * by_c, t0r * by_cc, t1r * by_rc], axis=0)
    imaginary = jnp.concatenate([t1r * by_r, t0r * by_c, t0i * by_cc, t1i * by_rc], axis=0)
    high, low = split(jnp.concatenate([real, imaginary], axis=1))
    table = table_ref[0]
    top, rest = table[: 2 * LANES], table[2 * LANES :]
    form = (((1,), (1,)), ((), ()))
    total = lax.dot_general(high, top, form, preferred_element_type=F32)
    total += lax.dot_general(high, rest, form, preferred_element_type=F32)
    total += lax.dot_general(low, top, form, preferred_element_type=F32)
    out_ref[0, 0] = total.reshape(out_ref.shape[2:])


def field_factors(length):
    bins = column_bins(length).astype(np.float64)
    wave = 2 * np.pi / length
    scale = -2.0 / (4 * np.pi**2)
    weight = np.ones_like(bins)
    weight[0] = 2.0
    weight[0, 0] = 1.0
    factor = np.zeros((bins.shape[0], TILE, LANES))
    factor[:, 0] = scale * wave * weight
    factor[:, 1] = scale * wave * bins * weight
    factor[:, 2] = -scale * wave * wave * bins * bins * weight
    factor[:, 3] = -scale * wave * wave * bins * weight
    return factor.astype(np.float32)


def back_over_lanes(returned, table, factors, begin):
    devices, count, own, width = returned.shape
    owned = table.shape[0] // devices
    slot = lambda d, i: (d * owned + begin + i, 0, 0)
    return pl.pallas_call(
        back_kernel,
        grid=(devices, count),
        in_specs=[
            pl.BlockSpec((1, 1, own, width), lambda d, i: (d, i, 0, 0)),
            pl.BlockSpec((1,) + table.shape[1:], slot),
            pl.BlockSpec((1,) + factors.shape[1:], slot),
        ],
        out_specs=pl.BlockSpec((1, 1, 4, own, 2 * LANES), lambda d, i: (d, i, 0, 0, 0)),
        out_shape=jax.ShapeDtypeStruct((devices, count, 4, own, 2 * LANES), F32),
        compiler_params=params(),
        cost_estimate=pl.CostEstimate(
            flops=6 * devices * count * 4 * own * 4 * LANES * LANES,
            bytes_accessed=devices * count * (12 * own * width + 8 * LANES * LANES),
            transcendentals=0,
        ),
        name="fields_lanes",
    )(returned, table, factors)


def advance_kernel(weight_ref, *refs):
    parts, (base_ref, state_ref, out_ref, field_ref) = refs[:-4], refs[-4:]
    devices = parts[0].shape[0]
    length = base_ref.shape[1]
    groups = length // LANES
    places = [
        (part, device, index)
        for device in range(devices)
        for part in parts
        for index in range(part.shape[1])
    ]

    def transform(field, carry):
        bins = []
        for part, device, index in places:
            bins.append(
                (part[device, index, field, :, :LANES], part[device, index, field, :, LANES:])
            )
        bins.append((bins[0][1], None))
        bins[0] = (bins[0][0], None)
        for u, block in enumerate(ifft_real(bins, groups)):
            field_ref[field, :, u * LANES : (u + 1) * LANES] = block
        return carry

    lax.fori_loop(0, 4, transform, 0)
    weight = weight_ref[0]

    def step(u, carry):
        at = pl.ds(pl.multiple_of(u * LANES, LANES), LANES)
        alpha_r, alpha_c, cc, rc = (field_ref[n, :, at] for n in range(4))
        rr = base_ref[:, at] - cc
        rr, cc, rc = weight * rr, weight * cc, weight * rc
        ul, ur, ll, lr = (state_ref[n, :, at] for n in range(2, 6))
        out_ref[0, :, at] = state_ref[0, :, at] - weight * alpha_r
        out_ref[1, :, at] = state_ref[1, :, at] - weight * alpha_c
        out_ref[2, :, at] = ul - (rr * ul + rc * ll)
        out_ref[3, :, at] = ur - (rr * ur + rc * lr)
        out_ref[4, :, at] = ll - (rc * ul + cc * ll)
        out_ref[5, :, at] = lr - (rc * ur + cc * lr)
        return carry

    lax.fori_loop(0, groups, step, 0)


def advance(weight, parts, base, state):
    devices, _, fields, own, width = parts[0].shape
    length = base.shape[1]
    return pl.pallas_call(
        advance_kernel,
        grid=(own // TILE,),
        in_specs=[pl.BlockSpec(memory_space=pltpu.SMEM)]
        + [
            pl.BlockSpec(
                (devices, part.shape[1], fields, TILE, width), lambda i: (0, 0, 0, i, 0)
            )
            for part in parts
        ]
        + [
            pl.BlockSpec((TILE, length), lambda i: (i, 0)),
            pl.BlockSpec((6, TILE, length), lambda i: (0, i, 0)),
        ],
        out_specs=pl.BlockSpec((6, TILE, length), lambda i: (0, i, 0)),
        out_shape=jax.ShapeDtypeStruct((6, own, length), F32),
        scratch_shapes=[pltpu.VMEM((fields, TILE, length), F32)],
        compiler_params=params(),
        cost_estimate=pl.CostEstimate(
            flops=100 * own * length, bytes_accessed=72 * own * length, transcendentals=0
        ),
        name="ray_step",
    )(weight, *parts, base, state)


def column_totals(sums):
    length = sums.shape[1]
    own = jnp.stack([jnp.sum(sums, axis=0), jnp.sum(sums[0::2] - sums[1::2], axis=0)])
    return lax.psum(own, ("row", "col")) / length


def curvature_sum(field, totals):
    rows, length = field.shape
    sign = jnp.where(jnp.arange(length) % 2 == 0, 1.0, -1.0).astype(F32)
    own = field.reshape(rows // STRIDE, STRIDE, length)[:, 0].astype(F32)
    whole, alternating = totals
    mean = jnp.mean(whole)
    both = jnp.mean(alternating * sign)
    by_row = jnp.mean(own * sign, axis=1, keepdims=True)
    return 2.0 * (own - sign * by_row - alternating + sign * both - mean)


def parted(owned):
    sizes = [1] * owned if owned < 4 else [1] + [2] * (owned // 2 - 1) + [1] * (1 + owned % 2)
    begins = [sum(sizes[:index]) for index in range(len(sizes))]
    return list(zip(begins, sizes))[::-1]


def passed_along(value, axis, steps):
    count = lax.axis_size(axis)
    leading, last = (max(0, -steps), min(count, count - steps))
    return lax.ppermute(value, axis, [(source, source + steps) for source in range(leading, last)])


def body(convergence, lens_weight, rays_in):
    planes = lax.axis_size("row")
    devices = lax.axis_size("col")
    _, rows, length = convergence.shape
    own = rows // STRIDE
    slots = length // LANES // 2
    owned = slots // devices
    runs = parted(owned)
    pieces = len(runs)
    field = convergence[0]
    table = jnp.asarray(column_table(length))
    tables = [jnp.asarray(t) for t in ray_tables(length // STRIDE, own * devices, length)]
    factors = jnp.asarray(field_factors(length))
    grouped, sums = over_groups(field)
    totals = column_totals(sums)
    place = jnp.stack([lax.axis_index("row"), lax.axis_index("col") * owned]).astype(jnp.int32)

    def send(step, *after):
        begin, count = runs[step]
        held = lax.optimization_barrier((grouped, *after))[0]
        return over_lanes(held, table, devices, begin, count)

    def exchange(value):
        return lax.all_to_all(value, "col", split_axis=0, concat_axis=0, tiled=True)

    sent = {step: send(step) for step in range(min(2, pieces))}
    arrived = {}
    for step in range(pieces):
        arrived[step] = exchange(sent[step])
        if step + 2 < pieces:
            sent[step + 2] = send(step + 2, arrived[step])
    summed = {}
    for step, (begin, count) in enumerate(runs):
        held = arrived[step]
        if step + 2 < pieces:
            held = lax.optimization_barrier((held, sent[step + 2]))[0]
        held = held.reshape(devices, count, STRIDE, own, 2 * LANES)
        shift = jnp.asarray(np.array([0, begin], np.int32))
        mean = None
        if begin == 0:
            late = lax.optimization_barrier((totals, arrived[step]))[0]
            mean = jnp.mean(late[0]).reshape(1)
        partial = to_rays(place + shift, mean, held, tables, planes)
        summed[step] = lax.psum_scatter(partial, "row", scatter_dimension=0, tiled=True)[0]
    done = {}
    for step, (begin, _) in enumerate(runs):
        held = summed[step]
        if step == pieces - 1:
            held = lax.optimization_barrier((held, *done.values()))[0]
        done[begin] = back_over_lanes(exchange(held), table, factors, begin)
    parts = [done[begin] for begin in sorted(done)]
    base = curvature_sum(field, late)

    def run_local(start):
        return advance(lens_weight, parts, base, start)[None]

    shell_index = lax.axis_index("shell")
    outputs = run_local(rays_in)
    for group in range(1, lax.axis_size("shell")):
        received = passed_along(outputs[-1], "shell", 1)
        outputs = jnp.where(shell_index == group, run_local(received), outputs)
    return outputs


def solution(mesh):
    in_specs = (P("shell", ("row", "col"), None), P("shell"), P(None, ("row", "col"), None))
    out_specs = P("shell", None, ("row", "col"), None)
    return jax.shard_map(body, mesh=mesh, in_specs=in_specs, out_specs=out_specs, check_vma=False)
```

```python
import functools
import math

import jax
import jax.numpy as jnp
import numpy as np
from jax import lax
from jax.experimental import pallas as pl
from jax.experimental.pallas import tpu as pltpu
from jax.sharding import PartitionSpec as P

STRIDE = 16
LANES = 128
TILE = 8
VMEM = 56 * 2**20
F32 = jnp.float32
BF16 = jnp.bfloat16


def plus(a, b):
    return b if a is None else a if b is None else a + b


def minus(a, b):
    return a if b is None else -b if a is None else a - b


def turned(value, numerator, denominator):
    numerator %= denominator
    real, imaginary = value
    eighth = 8 * numerator / denominator
    if eighth == 0:
        return value
    if eighth == 2:
        return (None if imaginary is None else -imaginary, real)
    if eighth == 4:
        return (-real, None if imaginary is None else -imaginary)
    if eighth == 6:
        return (imaginary, None if real is None else -real)
    cosine = math.cos(2 * math.pi * numerator / denominator)
    sine = math.sin(2 * math.pi * numerator / denominator)
    if real is None:
        return (imaginary * -sine, imaginary * cosine)
    if imaginary is None:
        return (real * cosine, real * sine)
    if eighth in (1, 3, 5, 7):
        scale = math.sqrt(0.5)
        if eighth == 1:
            return ((real - imaginary) * scale, (real + imaginary) * scale)
        if eighth == 3:
            return ((real + imaginary) * -scale, (real - imaginary) * scale)
        if eighth == 5:
            return ((imaginary - real) * scale, (real + imaginary) * -scale)
        return ((real + imaginary) * scale, (imaginary - real) * scale)
    return (real * cosine - imaginary * sine, real * sine + imaginary * cosine)


def c_add(a, b):
    return (plus(a[0], b[0]), plus(a[1], b[1]))


def c_sub(a, b):
    return (minus(a[0], b[0]), minus(a[1], b[1]))


def conj(a):
    return (a[0], None if a[1] is None else -a[1])


def fft_complex(values):
    count = len(values)
    if count == 1:
        return list(values)
    even, odd = fft_complex(values[0::2]), fft_complex(values[1::2])
    out = [None] * count
    for k in range(count // 2):
        term = turned(odd[k], -k, count)
        out[k] = c_add(even[k], term)
        out[k + count // 2] = c_sub(even[k], term)
    return out


def fft_real(values):
    count = len(values)
    if count == 1:
        return [(values[0], None)]
    if count == 2:
        return [(values[0] + values[1], None), (values[0] - values[1], None)]
    even, odd = fft_real(values[0::2]), fft_real(values[1::2])
    out = [None] * (count // 2 + 1)
    for k in range(count // 4 + 1):
        term = turned(odd[k], -k, count)
        out[k] = c_add(even[k], term)
        if k < count // 4:
            low = c_sub(even[k], term)
            real, imaginary = low
            if imaginary is not None:
                imaginary = term[1] - even[k][1] if even[k][1] is not None else term[1]
            out[count // 2 - k] = (real, imaginary)
    return out


def ifft_real(values, count):
    if count == 2:
        return [values[0][0] + values[1][0], values[0][0] - values[1][0]]
    even, odd = [], []
    for k in range(count // 4 + 1):
        a, b = values[k], values[count // 2 - k]
        if k == count // 4:
            even.append((a[0] + a[0], None))
            odd.append((-(a[1] + a[1]), None))
        elif k == 0:
            even.append((a[0] + b[0], None))
            odd.append((a[0] - b[0], None))
        else:
            even.append((a[0] + b[0], a[1] - b[1]))
            odd.append(turned((a[0] - b[0], a[1] + b[1]), k, count))
    out = [None] * count
    out[0::2] = ifft_real(even, count // 2)
    out[1::2] = ifft_real(odd, count // 2)
    return out


def halves(table):
    table = np.asarray(table, np.float32)
    high = table.astype(jnp.bfloat16)
    low = (table - high.astype(np.float32)).astype(jnp.bfloat16)
    return high, low


def column_bins(length):
    groups = length // LANES
    slot = np.arange(groups // 2)[:, None]
    lane = np.arange(LANES)[None, :]
    bins = slot + groups * lane
    bins = np.where(bins >= length // 2, bins - length, bins)
    half = LANES // 2
    bins[0] = np.where(lane[0] < half, groups * lane[0], groups // 2 + groups * (lane[0] - half))
    return bins


def column_table(length):
    bins = column_bins(length)
    slots = bins.shape[0]
    angle = 2 * np.pi / length * (bins[:, None, :] * np.arange(LANES)[None, :, None] % length)
    cosine, sine = np.cos(angle), np.sin(angle)
    table = np.zeros((slots, 2 * LANES, 2 * LANES))
    table[:, :LANES, :LANES] = cosine
    table[:, :LANES, LANES:] = -sine
    table[:, LANES:, :LANES] = sine
    table[:, LANES:, LANES:] = cosine
    half = LANES // 2
    first = np.zeros((2 * LANES, 2 * LANES))
    for begin, rows in ((0, slice(0, LANES)), (half, slice(LANES, 2 * LANES))):
        lanes = slice(begin, begin + half)
        first[rows, begin : begin + half] = cosine[0][:, lanes]
        first[rows, LANES + begin : LANES + begin + half] = -sine[0][:, lanes]
    table[0] = first
    high, low = halves(table)
    return np.concatenate([high, low], axis=1)


def ray_tables(rays, plane_rays, length):
    pairs = rays // 2
    rows = pairs + TILE
    order = np.arange(rows)
    angle = 2 * np.pi / rays * (order[:, None] * np.arange(plane_rays)[None, :] % rays)
    keep = (order <= pairs)[:, None]
    forward = np.concatenate([np.where(keep, np.cos(angle), 0), np.where(keep, -np.sin(angle), 0)])
    high, low = halves(forward)
    forward = np.concatenate([high, low, high], axis=1)
    turn = 2 * np.pi / length * (order[:, None] * np.arange(STRIDE)[None, :] % length)
    twist = np.zeros((rows, LANES), np.float32)
    twist[:, :STRIDE] = np.cos(turn)
    twist[:, STRIDE : 2 * STRIDE] = -np.sin(turn)
    angle = 2 * np.pi / rays * (np.arange(rays)[:, None] * np.arange(pairs)[None, :] % rays)
    cosine = np.cos(angle)
    cosine[:, 0] = 0.5
    backward = np.concatenate([cosine, np.sin(angle)], axis=1)
    high, low = halves(backward)
    return forward, twist, np.concatenate([high, low], axis=1)


def split(value):
    high = value.astype(BF16)
    return high, (value - high.astype(F32)).astype(BF16)


def dot(left, right):
    return jnp.dot(left, right, preferred_element_type=F32)


def params():
    return pltpu.CompilerParams(vmem_limit_bytes=VMEM)


def groups_kernel(x_ref, y_ref, sum_ref):
    rows, length = x_ref.shape
    groups = length // LANES

    @pl.when(pl.program_id(0) == 0)
    def _():
        sum_ref[...] = jnp.zeros_like(sum_ref)

    def step(index, carry):
        first = pl.multiple_of(index * 2 * TILE, 2 * TILE)
        for half in range(2):
            blocks = []
            for u in range(groups):
                lanes = slice(u * LANES, (u + 1) * LANES)
                block = x_ref[pl.ds(first, 2 * TILE), lanes].astype(F32)
                block = block[half * TILE : (half + 1) * TILE]
                sum_ref[:, lanes] += block
                blocks.append(block)
            bins = fft_real(blocks)
            place = pl.ds(pl.multiple_of(first + half * TILE, TILE), TILE)
            for slot in range(groups // 2):
                real, imaginary = bins[slot]
                if slot == 0:
                    imaginary = bins[groups // 2][0]
                y_ref[slot, 0, place] = real
                y_ref[slot, 1, place] = imaginary
        return carry

    lax.fori_loop(0, rows // (2 * TILE), step, 0)


def over_groups(field):
    rows, length = field.shape
    slots = length // LANES // 2
    step = min(rows, 32)
    return pl.pallas_call(
        groups_kernel,
        grid=(rows // step,),
        in_specs=[pl.BlockSpec((step, length), lambda i: (i, 0))],
        out_specs=[
            pl.BlockSpec((slots, 2, step, LANES), lambda i: (0, 0, i, 0)),
            pl.BlockSpec((TILE, length), lambda i: (0, 0)),
        ],
        out_shape=[
            jax.ShapeDtypeStruct((slots, 2, rows, LANES), F32),
            jax.ShapeDtypeStruct((TILE, length), F32),
        ],
        compiler_params=params(),
        cost_estimate=pl.CostEstimate(
            flops=20 * rows * length, bytes_accessed=6 * rows * length, transcendentals=0
        ),
        name="column_groups",
    )(field)


def lanes_kernel(y_ref, table_ref, out_ref):
    own = y_ref.shape[3] // STRIDE
    for d in range(y_ref.shape[0]):
        sides = []
        for side in range(2):
            pieces = [y_ref[d, 0, side, pl.ds(s, own, stride=STRIDE), :] for s in range(STRIDE)]
            sides.append(jnp.concatenate(pieces, axis=0))
        high, low = split(jnp.concatenate(sides, axis=1))
        table = table_ref[d, 0]
        top, rest = table[: 2 * LANES], table[2 * LANES :]
        out_ref[d, 0] = dot(
            jnp.concatenate([high, high, low], axis=1), jnp.concatenate([top, rest, top], axis=0)
        )


def over_lanes(grouped, table, begin, count):
    devices, owned, _, rows, lanes = grouped.shape
    width = 2 * lanes
    step = math.gcd(devices, 2)
    return pl.pallas_call(
        lanes_kernel,
        grid=(devices // step, count),
        in_specs=[
            pl.BlockSpec((step, 1, 2, rows, lanes), lambda d, i: (d, begin + i, 0, 0, 0)),
            pl.BlockSpec((step, 1, 2 * width, width), lambda d, i: (d, begin + i, 0, 0)),
        ],
        out_specs=pl.BlockSpec((step, 1, rows, width), lambda d, i: (d, i, 0, 0)),
        out_shape=jax.ShapeDtypeStruct((devices, count, rows, width), F32),
        compiler_params=params(),
        cost_estimate=pl.CostEstimate(
            flops=6 * devices * count * rows * width * width,
            bytes_accessed=8 * devices * count * rows * width,
            transcendentals=0,
        ),
        name="column_lanes",
    )(grouped, table)


def rays_kernel(has_mean, place_ref, mean_ref, x_ref, forward_ref, twist_ref, backward_ref, out_ref, cos_ref, sin_ref,
                pq_ref, ab_ref, high_ref, low_ref):
    sources, _, _, own, width = x_ref.shape
    planes = out_ref.shape[0]
    plane_rays = sources * own
    rays = planes * plane_rays
    pairs = rays // 2
    rows = pairs + TILE
    length = rays * STRIDE
    half = length // 2
    groups = length // LANES

    @pl.when(pl.program_id(0) == 0)
    def _():
        for s in range(STRIDE):
            cos_ref[s] = jnp.broadcast_to(twist_ref[:, s : s + 1], (rows, LANES))
            sin_ref[s] = jnp.broadcast_to(
                twist_ref[:, STRIDE + s : STRIDE + s + 1], (rows, LANES)
            )

    if has_mean:
        at_mean = lax.broadcasted_iota(jnp.int32, (1, width), 1) == 0
        at_mean = jnp.logical_and(at_mean, place_ref[1] + pl.program_id(0) == 0)
        offset = jnp.where(at_mean, mean_ref[0] * float(length), 0.0)

    def forward(s, carry):
        value = x_ref[:, 0, s].reshape(plane_rays, width)
        if has_mean:
            value = value - offset
        high, low = split(value)
        pq_ref[s] = dot(forward_ref[...], jnp.concatenate([high, high, low], axis=0))
        return carry

    lax.fori_loop(0, STRIDE, forward, 0)

    slot = place_ref[1] + pl.program_id(0)
    lane = lax.broadcasted_iota(jnp.int32, (TILE, LANES), 1)
    bins = slot + groups * lane
    bins = jnp.where(bins >= half, bins - length, bins)
    middle = LANES // 2
    first = jnp.where(lane < middle, groups * lane, groups // 2 + groups * (lane - middle))
    bins = jnp.where(slot == 0, first, bins).astype(F32)
    bins_squared = bins * bins
    sublane = lax.broadcasted_iota(jnp.int32, (TILE, LANES), 0)

    def filtered(block, carry):
        base = pl.multiple_of(block * TILE, TILE)
        at_p = pl.ds(base, TILE)
        at_q = pl.ds(pl.multiple_of(rows + base, TILE), TILE)
        order = (sublane + base).astype(F32)
        weights, wave_weights = [], []
        for a in range(STRIDE):
            wave = order + float(a * rays - (length if a >= STRIDE // 2 else 0))
            squared = wave * wave + bins_squared
            if a == 0:
                squared_safe = jnp.where(squared > 0.0, squared, 1.0)
            else:
                squared_safe = squared
            inverse = pl.reciprocal(squared_safe, approx=True)
            inverse = inverse * (2.0 - squared_safe * inverse)
            inverse = inverse * (2.0 - squared_safe * inverse)
            if a == 0:
                inverse = jnp.where(squared > 0.0, inverse, 0.0)
            if a == STRIDE // 2:
                inverse = jnp.where(order > 0.0, inverse, 0.0)
            weights.append(inverse)
            wave_weights.append(inverse * wave)
        sums = []
        for side in range(2):
            values = []
            for s in range(STRIDE):
                pr, pi = pq_ref[s, at_p, :LANES], pq_ref[s, at_p, LANES:]
                qr, qi = pq_ref[s, at_q, :LANES], pq_ref[s, at_q, LANES:]
                real, imaginary = (pr - qi, pi + qr) if side == 0 else (pr + qi, qr - pi)
                if s > 0:
                    cosine, sine = cos_ref[s, at_p], sin_ref[s, at_p]
                    real, imaginary = (
                        real * cosine - imaginary * sine,
                        real * sine + imaginary * cosine,
                    )
                values.append((real, imaginary))
            spectrum = fft_complex(values)
            for chosen in (weights, wave_weights):
                for which in range(2):
                    total = spectrum[0][which] * chosen[0]
                    for a in range(1, STRIDE):
                        total = total + spectrum[a][which] * chosen[a]
                    sums.append(total)
        a0r, a0i, a1r, a1i, b0r, b0i, b1r, b1i = sums
        even = (a0r + b0r, a0i - b0i, a1r - b1r, a1i + b1i)
        odd = (a0r - b0r, a0i + b0i, a1r + b1r, a1i - b1i)
        for index, value in enumerate(even):
            ab_ref[0, at_p, index * LANES : (index + 1) * LANES] = value
        for index, value in enumerate((-odd[1], odd[0], -odd[3], odd[2])):
            ab_ref[1, at_p, index * LANES : (index + 1) * LANES] = value
        return carry

    lax.fori_loop(0, rows // TILE, filtered, 0)

    for side in range(2):
        high, low = split(ab_ref[side, :pairs])
        high_ref[side * pairs : (side + 1) * pairs] = high
        low_ref[side * pairs : (side + 1) * pairs] = low
    last = ab_ref[0, pairs : pairs + TILE][:1] * 0.5
    parity = lax.broadcasted_iota(jnp.int32, (plane_rays, 4 * LANES), 0) % 2
    tail = jnp.where(parity == 0, last, -last)

    def backward(shift, carry):
        at = pl.ds(pl.multiple_of(shift * plane_rays, plane_rays), plane_rays)
        total = dot(backward_ref[at, :rays], high_ref[...])
        total += dot(backward_ref[at, rays:], high_ref[...])
        total += dot(backward_ref[at, :rays], low_ref[...])
        plane = lax.rem(place_ref[0] + shift, planes)
        out_ref[plane, :, 0] = (total + tail).reshape(sources, own, 4 * LANES)
        return carry

    lax.fori_loop(0, planes, backward, 0)


def to_rays(place, mean, arrived, tables, planes):
    sources, count, strides, own, width = arrived.shape
    forward, twist, backward = tables
    rays = planes * sources * own
    rows = rays // 2 + TILE

    def whole(array):
        return pl.BlockSpec(
            array.shape, lambda i, place: (0, 0), pipeline_mode=pl.Buffered(1)
        )

    return pl.pallas_call(
        functools.partial(rays_kernel, mean is not None),
        grid_spec=pltpu.PrefetchScalarGridSpec(
            num_scalar_prefetch=1,
            grid=(count,),
            in_specs=[
                pl.BlockSpec(memory_space=pltpu.SMEM),
                pl.BlockSpec(
                    (sources, 1, strides, own, width), lambda i, place: (0, i, 0, 0, 0)
                ),
                whole(forward),
                whole(twist),
                whole(backward),
            ],
            out_specs=pl.BlockSpec(
                (planes, sources, 1, own, 4 * LANES), lambda i, place: (0, 0, i, 0, 0)
            ),
            scratch_shapes=[
                pltpu.VMEM((STRIDE, rows, LANES), F32),
                pltpu.VMEM((STRIDE, rows, LANES), F32),
                pltpu.VMEM((STRIDE, 2 * rows, width), F32),
                pltpu.VMEM((2, rows, 4 * LANES), F32),
                pltpu.VMEM((rays, 4 * LANES), BF16),
                pltpu.VMEM((rays, 4 * LANES), BF16),
            ],
        ),
        out_shape=jax.ShapeDtypeStruct((planes, sources, count, own, 4 * LANES), F32),
        compiler_params=params(),
        cost_estimate=pl.CostEstimate(
            flops=8 * count * (6 * STRIDE * 2 * rows * sources * own * width
                           + 6 * rays * rays * 4 * LANES),
            bytes_accessed=4 * arrived.size + 16 * count * rays * LANES,
            transcendentals=0,
        ),
        name="ray_rows",
    )(place, jnp.zeros(1, F32) if mean is None else mean, arrived, forward, twist, backward)


def back_kernel(t_ref, table_ref, factor_ref, out_ref):
    form = (((1,), (1,)), ((), ()))
    for d in range(t_ref.shape[0]):
        t = t_ref[d, 0]
        t0r, t0i, t1r, t1i = (t[:, n * LANES : (n + 1) * LANES] for n in range(4))
        factor = factor_ref[d, 0]
        by_r, by_c, by_cc, by_rc = (factor[n : n + 1] for n in range(4))
        real = jnp.concatenate([-t1i * by_r, -t0i * by_c, t0r * by_cc, t1r * by_rc], axis=0)
        imaginary = jnp.concatenate([t1r * by_r, t0r * by_c, t0i * by_cc, t1i * by_rc], axis=0)
        high, low = split(jnp.concatenate([real, imaginary], axis=1))
        table = table_ref[d, 0]
        top, rest = table[: 2 * LANES], table[2 * LANES :]
        total = lax.dot_general(
            jnp.concatenate([high, high, low], axis=1),
            jnp.concatenate([top, rest, top], axis=1),
            form,
            preferred_element_type=F32,
        )
        out_ref[d, 0] = total.reshape(out_ref.shape[2:])


def field_factors(length):
    bins = column_bins(length).astype(np.float64)
    wave = 2 * np.pi / length
    scale = -2.0 / (4 * np.pi**2)
    weight = np.ones_like(bins)
    weight[0] = 2.0
    weight[0, 0] = 1.0
    factor = np.zeros((bins.shape[0], TILE, LANES))
    factor[:, 0] = scale * wave * weight
    factor[:, 1] = scale * wave * bins * weight
    factor[:, 2] = -scale * wave * wave * bins * bins * weight
    factor[:, 3] = -scale * wave * wave * bins * weight
    return factor.astype(np.float32)


def back_over_lanes(returned, table, factors, begin):
    devices, count, own, width = returned.shape
    step = math.gcd(devices, 4)
    return pl.pallas_call(
        back_kernel,
        grid=(devices // step, count),
        in_specs=[
            pl.BlockSpec((step, 1, own, width), lambda d, i: (d, i, 0, 0)),
            pl.BlockSpec((step, 1) + table.shape[2:], lambda d, i: (d, begin + i, 0, 0)),
            pl.BlockSpec((step, 1) + factors.shape[2:], lambda d, i: (d, begin + i, 0, 0)),
        ],
        out_specs=pl.BlockSpec((step, 1, 4, own, 2 * LANES), lambda d, i: (d, i, 0, 0, 0)),
        out_shape=jax.ShapeDtypeStruct((devices, count, 4, own, 2 * LANES), F32),
        compiler_params=params(),
        cost_estimate=pl.CostEstimate(
            flops=6 * devices * count * 4 * own * 4 * LANES * LANES,
            bytes_accessed=devices * count * (12 * own * width + 8 * LANES * LANES),
            transcendentals=0,
        ),
        name="fields_lanes",
    )(returned, table, factors)


def advance_kernel(weight_ref, *refs):
    parts, (base_ref, state_ref, out_ref, field_ref) = refs[:-4], refs[-4:]
    devices = parts[0].shape[0]
    length = base_ref.shape[1]
    groups = length // LANES
    places = [
        (part, device, index)
        for device in range(devices)
        for part in parts
        for index in range(part.shape[1])
    ]

    def transform(field, carry):
        bins = []
        for part, device, index in places:
            bins.append(
                (part[device, index, field, :, :LANES], part[device, index, field, :, LANES:])
            )
        bins.append((bins[0][1], None))
        bins[0] = (bins[0][0], None)
        for u, block in enumerate(ifft_real(bins, groups)):
            field_ref[field, :, u * LANES : (u + 1) * LANES] = block
        return carry

    lax.fori_loop(0, 4, transform, 0)
    weight = weight_ref[0]

    def step(u, carry):
        at = pl.ds(pl.multiple_of(u * LANES, LANES), LANES)
        alpha_r, alpha_c, cc, rc = (field_ref[n, :, at] for n in range(4))
        rr = base_ref[:, at] - cc
        rr, cc, rc = weight * rr, weight * cc, weight * rc
        ul, ur, ll, lr = (state_ref[n, :, at] for n in range(2, 6))
        out_ref[0, :, at] = state_ref[0, :, at] - weight * alpha_r
        out_ref[1, :, at] = state_ref[1, :, at] - weight * alpha_c
        out_ref[2, :, at] = ul - (rr * ul + rc * ll)
        out_ref[3, :, at] = ur - (rr * ur + rc * lr)
        out_ref[4, :, at] = ll - (rc * ul + cc * ll)
        out_ref[5, :, at] = lr - (rc * ur + cc * lr)
        return carry

    lax.fori_loop(0, groups, step, 0)


def advance(weight, parts, base, state):
    devices, _, fields, own, width = parts[0].shape
    length = base.shape[1]
    return pl.pallas_call(
        advance_kernel,
        grid=(own // TILE,),
        in_specs=[pl.BlockSpec(memory_space=pltpu.SMEM)]
        + [
            pl.BlockSpec(
                (devices, part.shape[1], fields, TILE, width), lambda i: (0, 0, 0, i, 0)
            )
            for part in parts
        ]
        + [
            pl.BlockSpec((TILE, length), lambda i: (i, 0)),
            pl.BlockSpec((6, TILE, length), lambda i: (0, i, 0)),
        ],
        out_specs=pl.BlockSpec((6, TILE, length), lambda i: (0, i, 0)),
        out_shape=jax.ShapeDtypeStruct((6, own, length), F32),
        scratch_shapes=[pltpu.VMEM((fields, TILE, length), F32)],
        compiler_params=params(),
        cost_estimate=pl.CostEstimate(
            flops=100 * own * length, bytes_accessed=72 * own * length, transcendentals=0
        ),
        name="ray_step",
    )(weight, *parts, base, state)


def column_totals(sums):
    length = sums.shape[1]
    own = jnp.stack([jnp.sum(sums, axis=0), jnp.sum(sums[0::2] - sums[1::2], axis=0)])
    return lax.psum(own, ("row", "col")) / length


def curvature_sum(field, totals):
    rows, length = field.shape
    sign = jnp.where(jnp.arange(length) % 2 == 0, 1.0, -1.0).astype(F32)
    own = field.reshape(rows // STRIDE, STRIDE, length)[:, 0].astype(F32)
    whole, alternating = totals
    mean = jnp.mean(whole)
    both = jnp.mean(alternating * sign)
    by_row = jnp.mean(own * sign, axis=1, keepdims=True)
    return 2.0 * (own - sign * by_row - alternating + sign * both - mean)


def parted(owned):
    sizes = [1] * owned if owned < 4 else [1] + [2] * (owned // 2 - 1) + [1] * (1 + owned % 2)
    begins = [sum(sizes[:index]) for index in range(len(sizes))]
    return list(zip(begins, sizes))[::-1]


def passed_along(value, axis, steps):
    count = lax.axis_size(axis)
    leading, last = (max(0, -steps), min(count, count - steps))
    return lax.ppermute(value, axis, [(source, source + steps) for source in range(leading, last)])


def body(convergence, lens_weight, rays_in):
    planes = lax.axis_size("row")
    devices = lax.axis_size("col")
    _, rows, length = convergence.shape
    own = rows // STRIDE
    slots = length // LANES // 2
    owned = slots // devices
    runs = parted(owned)
    pieces = len(runs)
    field = convergence[0]
    table = jnp.asarray(column_table(length).reshape(devices, owned, 4 * LANES, 2 * LANES))
    tables = [jnp.asarray(t) for t in ray_tables(length // STRIDE, own * devices, length)]
    factors = jnp.asarray(field_factors(length).reshape(devices, owned, TILE, LANES))
    grouped, sums = over_groups(field)
    grouped = grouped.reshape(devices, owned, *grouped.shape[1:])
    totals = column_totals(sums)
    place = jnp.stack([lax.axis_index("row"), lax.axis_index("col") * owned]).astype(jnp.int32)

    def send(step, *after):
        begin, count = runs[step]
        held = lax.optimization_barrier((grouped, *after))[0]
        return over_lanes(held, table, begin, count)

    def exchange(value):
        return lax.all_to_all(value, "col", split_axis=0, concat_axis=0, tiled=True)

    sent = {step: send(step) for step in range(min(2, pieces))}
    arrived, partial, summed = {}, {}, {}
    for step, (begin, count) in enumerate(runs):
        arrived[step] = exchange(sent[step])
        if step + 2 < pieces:
            sent[step + 2] = send(step + 2, arrived[step])
        held = arrived[step]
        if step + 2 < pieces:
            held = lax.optimization_barrier((held, sent[step + 2]))[0]
        held = held.reshape(devices, count, STRIDE, own, 2 * LANES)
        shift = jnp.asarray(np.array([0, begin], np.int32))
        mean = None
        if begin == 0:
            late = lax.optimization_barrier((totals, arrived[step]))[0]
            mean = jnp.mean(late[0]).reshape(1)
        partial[step] = to_rays(place + shift, mean, held, tables, planes)
        summed[step] = lax.psum_scatter(
            partial[step], "row", scatter_dimension=0, tiled=True
        )[0]
    done = {}
    for step, (begin, _) in enumerate(runs):
        held = summed[step]
        if step == pieces - 1:
            held = lax.optimization_barrier((held, *done.values()))[0]
        done[begin] = back_over_lanes(exchange(held), table, factors, begin)
    parts = [done[begin] for begin in sorted(done)]
    base = curvature_sum(field, late)

    def run_local(start):
        return advance(lens_weight, parts, base, start)[None]

    shell_index = lax.axis_index("shell")
    outputs = run_local(rays_in)
    for group in range(1, lax.axis_size("shell")):
        received = passed_along(outputs[-1], "shell", 1)
        outputs = jnp.where(shell_index == group, run_local(received), outputs)
    return outputs


def solution(mesh):
    in_specs = (P("shell", ("row", "col"), None), P("shell"), P(None, ("row", "col"), None))
    out_specs = P("shell", None, ("row", "col"), None)
    return jax.shard_map(body, mesh=mesh, in_specs=in_specs, out_specs=out_specs, check_vma=False)
```

```python
import functools
import math

import jax
import jax.numpy as jnp
import numpy as np
from jax import lax
from jax.experimental import pallas as pl
from jax.experimental.pallas import tpu as pltpu
from jax.sharding import PartitionSpec as P

STRIDE = 16
LANES = 128
TILE = 8
VMEM = 56 * 2**20
F32 = jnp.float32
BF16 = jnp.bfloat16


def plus(a, b):
    return b if a is None else a if b is None else a + b


def minus(a, b):
    return a if b is None else -b if a is None else a - b


def turned(value, numerator, denominator):
    numerator %= denominator
    real, imaginary = value
    eighth = 8 * numerator / denominator
    if eighth == 0:
        return value
    if eighth == 2:
        return (None if imaginary is None else -imaginary, real)
    if eighth == 4:
        return (-real, None if imaginary is None else -imaginary)
    if eighth == 6:
        return (imaginary, None if real is None else -real)
    cosine = math.cos(2 * math.pi * numerator / denominator)
    sine = math.sin(2 * math.pi * numerator / denominator)
    if real is None:
        return (imaginary * -sine, imaginary * cosine)
    if imaginary is None:
        return (real * cosine, real * sine)
    if eighth in (1, 3, 5, 7):
        scale = math.sqrt(0.5)
        if eighth == 1:
            return ((real - imaginary) * scale, (real + imaginary) * scale)
        if eighth == 3:
            return ((real + imaginary) * -scale, (real - imaginary) * scale)
        if eighth == 5:
            return ((imaginary - real) * scale, (real + imaginary) * -scale)
        return ((real + imaginary) * scale, (imaginary - real) * scale)
    return (real * cosine - imaginary * sine, real * sine + imaginary * cosine)


def c_add(a, b):
    return (plus(a[0], b[0]), plus(a[1], b[1]))


def c_sub(a, b):
    return (minus(a[0], b[0]), minus(a[1], b[1]))


def conj(a):
    return (a[0], None if a[1] is None else -a[1])


def fft_complex(values):
    count = len(values)
    if count == 1:
        return list(values)
    even, odd = fft_complex(values[0::2]), fft_complex(values[1::2])
    out = [None] * count
    for k in range(count // 2):
        term = turned(odd[k], -k, count)
        out[k] = c_add(even[k], term)
        out[k + count // 2] = c_sub(even[k], term)
    return out


def fft_real(values):
    count = len(values)
    if count == 1:
        return [(values[0], None)]
    if count == 2:
        return [(values[0] + values[1], None), (values[0] - values[1], None)]
    even, odd = fft_real(values[0::2]), fft_real(values[1::2])
    out = [None] * (count // 2 + 1)
    for k in range(count // 4 + 1):
        term = turned(odd[k], -k, count)
        out[k] = c_add(even[k], term)
        if k < count // 4:
            low = c_sub(even[k], term)
            real, imaginary = low
            if imaginary is not None:
                imaginary = term[1] - even[k][1] if even[k][1] is not None else term[1]
            out[count // 2 - k] = (real, imaginary)
    return out


def ifft_real(values, count):
    if count == 2:
        return [values[0][0] + values[1][0], values[0][0] - values[1][0]]
    even, odd = [], []
    for k in range(count // 4 + 1):
        a, b = values[k], values[count // 2 - k]
        if k == count // 4:
            even.append((a[0] + a[0], None))
            odd.append((-(a[1] + a[1]), None))
        elif k == 0:
            even.append((a[0] + b[0], None))
            odd.append((a[0] - b[0], None))
        else:
            even.append((a[0] + b[0], a[1] - b[1]))
            odd.append(turned((a[0] - b[0], a[1] + b[1]), k, count))
    out = [None] * count
    out[0::2] = ifft_real(even, count // 2)
    out[1::2] = ifft_real(odd, count // 2)
    return out


def halves(table):
    table = np.asarray(table, np.float32)
    high = table.astype(jnp.bfloat16)
    low = (table - high.astype(np.float32)).astype(jnp.bfloat16)
    return high, low


def column_bins(length):
    groups = length // LANES
    slot = np.arange(groups // 2)[:, None]
    lane = np.arange(LANES)[None, :]
    bins = slot + groups * lane
    bins = np.where(bins >= length // 2, bins - length, bins)
    half = LANES // 2
    bins[0] = np.where(lane[0] < half, groups * lane[0], groups // 2 + groups * (lane[0] - half))
    return bins


def column_table(length):
    bins = column_bins(length)
    slots = bins.shape[0]
    angle = 2 * np.pi / length * (bins[:, None, :] * np.arange(LANES)[None, :, None] % length)
    cosine, sine = np.cos(angle), np.sin(angle)
    table = np.zeros((slots, 2 * LANES, 2 * LANES))
    table[:, :LANES, :LANES] = cosine
    table[:, :LANES, LANES:] = -sine
    table[:, LANES:, :LANES] = sine
    table[:, LANES:, LANES:] = cosine
    half = LANES // 2
    first = np.zeros((2 * LANES, 2 * LANES))
    for begin, rows in ((0, slice(0, LANES)), (half, slice(LANES, 2 * LANES))):
        lanes = slice(begin, begin + half)
        first[rows, begin : begin + half] = cosine[0][:, lanes]
        first[rows, LANES + begin : LANES + begin + half] = -sine[0][:, lanes]
    table[0] = first
    high, low = halves(table)
    return np.concatenate([high, low], axis=1)


def ray_tables(rays, plane_rays, length):
    pairs = rays // 2
    rows = pairs + TILE
    order = np.arange(rows)
    angle = 2 * np.pi / rays * (order[:, None] * np.arange(plane_rays)[None, :] % rays)
    keep = (order <= pairs)[:, None]
    forward = np.concatenate([np.where(keep, np.cos(angle), 0), np.where(keep, -np.sin(angle), 0)])
    high, low = halves(forward)
    forward = np.concatenate([high, low, high], axis=1)
    turn = 2 * np.pi / length * (order[:, None] * np.arange(STRIDE)[None, :] % length)
    twist = np.zeros((rows, LANES), np.float32)
    twist[:, :STRIDE] = np.cos(turn)
    twist[:, STRIDE : 2 * STRIDE] = -np.sin(turn)
    angle = 2 * np.pi / rays * (np.arange(rays)[:, None] * np.arange(pairs)[None, :] % rays)
    cosine = np.cos(angle)
    cosine[:, 0] = 0.5
    backward = np.concatenate([cosine, np.sin(angle)], axis=1)
    high, low = halves(backward)
    return forward, twist, np.concatenate([high, low], axis=1)


def split(value):
    high = value.astype(BF16)
    return high, (value - high.astype(F32)).astype(BF16)


def dot(left, right):
    return jnp.dot(left, right, preferred_element_type=F32)


def params():
    return pltpu.CompilerParams(vmem_limit_bytes=VMEM)


def groups_kernel(x_ref, y_ref, sum_ref):
    rows, length = x_ref.shape
    groups = length // LANES

    @pl.when(pl.program_id(0) == 0)
    def _():
        sum_ref[...] = jnp.zeros_like(sum_ref)

    def step(index, carry):
        first = pl.multiple_of(index * 2 * TILE, 2 * TILE)
        for half in range(2):
            blocks = []
            for u in range(groups):
                lanes = slice(u * LANES, (u + 1) * LANES)
                block = x_ref[pl.ds(first, 2 * TILE), lanes].astype(F32)
                block = block[half * TILE : (half + 1) * TILE]
                sum_ref[:, lanes] += block
                blocks.append(block)
            bins = fft_real(blocks)
            place = pl.ds(pl.multiple_of(first + half * TILE, TILE), TILE)
            for slot in range(groups // 2):
                real, imaginary = bins[slot]
                if slot == 0:
                    imaginary = bins[groups // 2][0]
                y_ref[slot, 0, place] = real
                y_ref[slot, 1, place] = imaginary
        return carry

    lax.fori_loop(0, rows // (2 * TILE), step, 0)


def over_groups(field):
    rows, length = field.shape
    slots = length // LANES // 2
    step = min(rows, 32)
    return pl.pallas_call(
        groups_kernel,
        grid=(rows // step,),
        in_specs=[pl.BlockSpec((step, length), lambda i: (i, 0))],
        out_specs=[
            pl.BlockSpec((slots, 2, step, LANES), lambda i: (0, 0, i, 0)),
            pl.BlockSpec((TILE, length), lambda i: (0, 0)),
        ],
        out_shape=[
            jax.ShapeDtypeStruct((slots, 2, rows, LANES), F32),
            jax.ShapeDtypeStruct((TILE, length), F32),
        ],
        compiler_params=params(),
        cost_estimate=pl.CostEstimate(
            flops=20 * rows * length, bytes_accessed=6 * rows * length, transcendentals=0
        ),
        name="column_groups",
    )(field)


def lanes_kernel(y_ref, table_ref, out_ref):
    own = y_ref.shape[3] // STRIDE
    for d in range(y_ref.shape[0]):
        sides = []
        for side in range(2):
            pieces = [y_ref[d, 0, side, pl.ds(s, own, stride=STRIDE), :] for s in range(STRIDE)]
            sides.append(jnp.concatenate(pieces, axis=0))
        high, low = split(jnp.concatenate(sides, axis=1))
        table = table_ref[d, 0]
        top, rest = table[: 2 * LANES], table[2 * LANES :]
        out_ref[d, 0] = dot(
            jnp.concatenate([high, high, low], axis=1), jnp.concatenate([top, rest, top], axis=0)
        )


def over_lanes(grouped, table, begin, count):
    devices, owned, _, rows, lanes = grouped.shape
    width = 2 * lanes
    step = math.gcd(devices, 2)
    return pl.pallas_call(
        lanes_kernel,
        grid=(devices // step, count),
        in_specs=[
            pl.BlockSpec((step, 1, 2, rows, lanes), lambda d, i: (d, begin + i, 0, 0, 0)),
            pl.BlockSpec((step, 1, 2 * width, width), lambda d, i: (d, begin + i, 0, 0)),
        ],
        out_specs=pl.BlockSpec((step, 1, rows, width), lambda d, i: (d, i, 0, 0)),
        out_shape=jax.ShapeDtypeStruct((devices, count, rows, width), F32),
        compiler_params=params(),
        cost_estimate=pl.CostEstimate(
            flops=6 * devices * count * rows * width * width,
            bytes_accessed=8 * devices * count * rows * width,
            transcendentals=0,
        ),
        name="column_lanes",
    )(grouped, table)


def rays_kernel(has_mean, place_ref, mean_ref, x_ref, forward_ref, twist_ref, backward_ref, out_ref, cos_ref, sin_ref,
                pq_ref, ab_ref, high_ref, low_ref):
    sources, _, _, own, width = x_ref.shape
    planes = out_ref.shape[0]
    plane_rays = sources * own
    rays = planes * plane_rays
    pairs = rays // 2
    rows = pairs + TILE
    length = rays * STRIDE
    half = length // 2
    groups = length // LANES

    @pl.when(pl.program_id(0) == 0)
    def _():
        for s in range(STRIDE):
            cos_ref[s] = jnp.broadcast_to(twist_ref[:, s : s + 1], (rows, LANES))
            sin_ref[s] = jnp.broadcast_to(
                twist_ref[:, STRIDE + s : STRIDE + s + 1], (rows, LANES)
            )

    if has_mean:
        at_mean = lax.broadcasted_iota(jnp.int32, (1, width), 1) == 0
        at_mean = jnp.logical_and(at_mean, place_ref[1] + pl.program_id(0) == 0)
        offset = jnp.where(at_mean, mean_ref[0] * float(length), 0.0)

    def forward(s, carry):
        value = x_ref[:, 0, s].reshape(plane_rays, width)
        if has_mean:
            value = value - offset
        high, low = split(value)
        pq_ref[s] = dot(forward_ref[...], jnp.concatenate([high, high, low], axis=0))
        return carry

    lax.fori_loop(0, STRIDE, forward, 0)

    slot = place_ref[1] + pl.program_id(0)
    lane = lax.broadcasted_iota(jnp.int32, (TILE, LANES), 1)
    bins = slot + groups * lane
    bins = jnp.where(bins >= half, bins - length, bins)
    middle = LANES // 2
    first = jnp.where(lane < middle, groups * lane, groups // 2 + groups * (lane - middle))
    bins = jnp.where(slot == 0, first, bins).astype(F32)
    bins_squared = bins * bins
    sublane = lax.broadcasted_iota(jnp.int32, (TILE, LANES), 0)

    def filtered(block, carry):
        base = pl.multiple_of(block * TILE, TILE)
        at_p = pl.ds(base, TILE)
        at_q = pl.ds(pl.multiple_of(rows + base, TILE), TILE)
        order = (sublane + base).astype(F32)
        weights, wave_weights = [], []
        for a in range(STRIDE):
            wave = order + float(a * rays - (length if a >= STRIDE // 2 else 0))
            squared = wave * wave + bins_squared
            if a == 0:
                squared_safe = jnp.where(squared > 0.0, squared, 1.0)
            else:
                squared_safe = squared
            inverse = pl.reciprocal(squared_safe, approx=True)
            inverse = inverse * (2.0 - squared_safe * inverse)
            if a == 0:
                inverse = jnp.where(squared > 0.0, inverse, 0.0)
            if a == STRIDE // 2:
                inverse = jnp.where(order > 0.0, inverse, 0.0)
            weights.append(inverse)
            wave_weights.append(inverse * wave)
        sums = []
        for side in range(2):
            values = []
            for s in range(STRIDE):
                pr, pi = pq_ref[s, at_p, :LANES], pq_ref[s, at_p, LANES:]
                qr, qi = pq_ref[s, at_q, :LANES], pq_ref[s, at_q, LANES:]
                real, imaginary = (pr - qi, pi + qr) if side == 0 else (pr + qi, qr - pi)
                if s > 0:
                    cosine, sine = cos_ref[s, at_p], sin_ref[s, at_p]
                    real, imaginary = (
                        real * cosine - imaginary * sine,
                        real * sine + imaginary * cosine,
                    )
                values.append((real, imaginary))
            spectrum = fft_complex(values)
            for chosen in (weights, wave_weights):
                for which in range(2):
                    total = spectrum[0][which] * chosen[0]
                    for a in range(1, STRIDE):
                        total = total + spectrum[a][which] * chosen[a]
                    sums.append(total)
        a0r, a0i, a1r, a1i, b0r, b0i, b1r, b1i = sums
        even = (a0r + b0r, a0i - b0i, a1r - b1r, a1i + b1i)
        odd = (a0r - b0r, a0i + b0i, a1r + b1r, a1i - b1i)
        for index, value in enumerate(even):
            ab_ref[0, at_p, index * LANES : (index + 1) * LANES] = value
        for index, value in enumerate((-odd[1], odd[0], -odd[3], odd[2])):
            ab_ref[1, at_p, index * LANES : (index + 1) * LANES] = value
        return carry

    lax.fori_loop(0, rows // TILE, filtered, 0)

    for side in range(2):
        high, low = split(ab_ref[side, :pairs])
        high_ref[side * pairs : (side + 1) * pairs] = high
        low_ref[side * pairs : (side + 1) * pairs] = low
    last = ab_ref[0, pairs : pairs + TILE][:1] * 0.5
    parity = lax.broadcasted_iota(jnp.int32, (plane_rays, 4 * LANES), 0) % 2
    tail = jnp.where(parity == 0, last, -last)

    def backward(shift, carry):
        at = pl.ds(pl.multiple_of(shift * plane_rays, plane_rays), plane_rays)
        total = dot(backward_ref[at, :rays], high_ref[...])
        total += dot(backward_ref[at, rays:], high_ref[...])
        total += dot(backward_ref[at, :rays], low_ref[...])
        plane = lax.rem(place_ref[0] + shift, planes)
        out_ref[plane, :, 0] = (total + tail).reshape(sources, own, 4 * LANES)
        return carry

    lax.fori_loop(0, planes, backward, 0)


def to_rays(place, mean, arrived, tables, planes):
    sources, count, strides, own, width = arrived.shape
    forward, twist, backward = tables
    rays = planes * sources * own
    rows = rays // 2 + TILE

    def whole(array):
        return pl.BlockSpec(
            array.shape, lambda i, place: (0, 0), pipeline_mode=pl.Buffered(1)
        )

    return pl.pallas_call(
        functools.partial(rays_kernel, mean is not None),
        grid_spec=pltpu.PrefetchScalarGridSpec(
            num_scalar_prefetch=1,
            grid=(count,),
            in_specs=[
                pl.BlockSpec(memory_space=pltpu.SMEM),
                pl.BlockSpec(
                    (sources, 1, strides, own, width), lambda i, place: (0, i, 0, 0, 0)
                ),
                whole(forward),
                whole(twist),
                whole(backward),
            ],
            out_specs=pl.BlockSpec(
                (planes, sources, 1, own, 4 * LANES), lambda i, place: (0, 0, i, 0, 0)
            ),
            scratch_shapes=[
                pltpu.VMEM((STRIDE, rows, LANES), F32),
                pltpu.VMEM((STRIDE, rows, LANES), F32),
                pltpu.VMEM((STRIDE, 2 * rows, width), F32),
                pltpu.VMEM((2, rows, 4 * LANES), F32),
                pltpu.VMEM((rays, 4 * LANES), BF16),
                pltpu.VMEM((rays, 4 * LANES), BF16),
            ],
        ),
        out_shape=jax.ShapeDtypeStruct((planes, sources, count, own, 4 * LANES), F32),
        compiler_params=params(),
        cost_estimate=pl.CostEstimate(
            flops=8 * count * (6 * STRIDE * 2 * rows * sources * own * width
                           + 6 * rays * rays * 4 * LANES),
            bytes_accessed=4 * arrived.size + 16 * count * rays * LANES,
            transcendentals=0,
        ),
        name="ray_rows",
    )(place, jnp.zeros(1, F32) if mean is None else mean, arrived, forward, twist, backward)


def back_kernel(t_ref, table_ref, factor_ref, out_ref):
    form = (((1,), (1,)), ((), ()))
    for d in range(t_ref.shape[0]):
        t = t_ref[d, 0]
        t0r, t0i, t1r, t1i = (t[:, n * LANES : (n + 1) * LANES] for n in range(4))
        factor = factor_ref[d, 0]
        by_r, by_c, by_cc, by_rc = (factor[n : n + 1] for n in range(4))
        real = jnp.concatenate([-t1i * by_r, -t0i * by_c, t0r * by_cc, t1r * by_rc], axis=0)
        imaginary = jnp.concatenate([t1r * by_r, t0r * by_c, t0i * by_cc, t1i * by_rc], axis=0)
        high, low = split(jnp.concatenate([real, imaginary], axis=1))
        table = table_ref[d, 0]
        top, rest = table[: 2 * LANES], table[2 * LANES :]
        total = lax.dot_general(
            jnp.concatenate([high, high, low], axis=1),
            jnp.concatenate([top, rest, top], axis=1),
            form,
            preferred_element_type=F32,
        )
        out_ref[d, 0] = total.reshape(out_ref.shape[2:])


def field_factors(length):
    bins = column_bins(length).astype(np.float64)
    wave = 2 * np.pi / length
    scale = -2.0 / (4 * np.pi**2)
    weight = np.ones_like(bins)
    weight[0] = 2.0
    weight[0, 0] = 1.0
    factor = np.zeros((bins.shape[0], TILE, LANES))
    factor[:, 0] = scale * wave * weight
    factor[:, 1] = scale * wave * bins * weight
    factor[:, 2] = -scale * wave * wave * bins * bins * weight
    factor[:, 3] = -scale * wave * wave * bins * weight
    return factor.astype(np.float32)


def back_over_lanes(returned, table, factors, begin):
    devices, count, own, width = returned.shape
    step = math.gcd(devices, 8)
    return pl.pallas_call(
        back_kernel,
        grid=(devices // step, count),
        in_specs=[
            pl.BlockSpec((step, 1, own, width), lambda d, i: (d, i, 0, 0)),
            pl.BlockSpec((step, 1) + table.shape[2:], lambda d, i: (d, begin + i, 0, 0)),
            pl.BlockSpec((step, 1) + factors.shape[2:], lambda d, i: (d, begin + i, 0, 0)),
        ],
        out_specs=pl.BlockSpec((step, 1, 4, own, 2 * LANES), lambda d, i: (d, i, 0, 0, 0)),
        out_shape=jax.ShapeDtypeStruct((devices, count, 4, own, 2 * LANES), F32),
        compiler_params=params(),
        cost_estimate=pl.CostEstimate(
            flops=6 * devices * count * 4 * own * 4 * LANES * LANES,
            bytes_accessed=devices * count * (12 * own * width + 8 * LANES * LANES),
            transcendentals=0,
        ),
        name="fields_lanes",
    )(returned, table, factors)


def advance_kernel(weight_ref, *refs):
    parts, (base_ref, state_ref, out_ref, field_ref) = refs[:-4], refs[-4:]
    devices = parts[0].shape[0]
    length = base_ref.shape[1]
    groups = length // LANES
    places = [
        (part, device, index)
        for device in range(devices)
        for part in parts
        for index in range(part.shape[1])
    ]

    def transform(field, carry):
        bins = []
        for part, device, index in places:
            bins.append(
                (part[device, index, field, :, :LANES], part[device, index, field, :, LANES:])
            )
        bins.append((bins[0][1], None))
        bins[0] = (bins[0][0], None)
        for u, block in enumerate(ifft_real(bins, groups)):
            field_ref[field, :, u * LANES : (u + 1) * LANES] = block
        return carry

    lax.fori_loop(0, 4, transform, 0)
    weight = weight_ref[0]

    def step(u, carry):
        at = pl.ds(pl.multiple_of(u * LANES, LANES), LANES)
        alpha_r, alpha_c, cc, rc = (field_ref[n, :, at] for n in range(4))
        rr = base_ref[:, at] - cc
        rr, cc, rc = weight * rr, weight * cc, weight * rc
        ul, ur, ll, lr = (state_ref[n, :, at] for n in range(2, 6))
        out_ref[0, :, at] = state_ref[0, :, at] - weight * alpha_r
        out_ref[1, :, at] = state_ref[1, :, at] - weight * alpha_c
        out_ref[2, :, at] = ul - (rr * ul + rc * ll)
        out_ref[3, :, at] = ur - (rr * ur + rc * lr)
        out_ref[4, :, at] = ll - (rc * ul + cc * ll)
        out_ref[5, :, at] = lr - (rc * ur + cc * lr)
        return carry

    lax.fori_loop(0, groups, step, 0)


def advance(weight, parts, base, state):
    devices, _, fields, own, width = parts[0].shape
    length = base.shape[1]
    return pl.pallas_call(
        advance_kernel,
        grid=(own // TILE,),
        in_specs=[pl.BlockSpec(memory_space=pltpu.SMEM)]
        + [
            pl.BlockSpec(
                (devices, part.shape[1], fields, TILE, width), lambda i: (0, 0, 0, i, 0)
            )
            for part in parts
        ]
        + [
            pl.BlockSpec((TILE, length), lambda i: (i, 0)),
            pl.BlockSpec((6, TILE, length), lambda i: (0, i, 0)),
        ],
        out_specs=pl.BlockSpec((6, TILE, length), lambda i: (0, i, 0)),
        out_shape=jax.ShapeDtypeStruct((6, own, length), F32),
        scratch_shapes=[pltpu.VMEM((fields, TILE, length), F32)],
        compiler_params=params(),
        cost_estimate=pl.CostEstimate(
            flops=100 * own * length, bytes_accessed=72 * own * length, transcendentals=0
        ),
        name="ray_step",
    )(weight, *parts, base, state)


def column_totals(sums):
    length = sums.shape[1]
    own = jnp.stack([jnp.sum(sums, axis=0), jnp.sum(sums[0::2] - sums[1::2], axis=0)])
    return lax.psum(own, ("row", "col")) / length


def curvature_sum(field, totals):
    rows, length = field.shape
    sign = jnp.where(jnp.arange(length) % 2 == 0, 1.0, -1.0).astype(F32)
    own = field.reshape(rows // STRIDE, STRIDE, length)[:, 0].astype(F32)
    whole, alternating = totals
    mean = jnp.mean(whole)
    both = jnp.mean(alternating * sign)
    by_row = jnp.mean(own * sign, axis=1, keepdims=True)
    return 2.0 * (own - sign * by_row - alternating + sign * both - mean)


def parted(owned):
    sizes = [1] * owned if owned < 4 else [1] + [2] * (owned // 2 - 1) + [1] * (1 + owned % 2)
    begins = [sum(sizes[:index]) for index in range(len(sizes))]
    return list(zip(begins, sizes))[::-1]


def passed_along(value, axis, steps):
    count = lax.axis_size(axis)
    leading, last = (max(0, -steps), min(count, count - steps))
    return lax.ppermute(value, axis, [(source, source + steps) for source in range(leading, last)])


def body(convergence, lens_weight, rays_in):
    planes = lax.axis_size("row")
    devices = lax.axis_size("col")
    _, rows, length = convergence.shape
    own = rows // STRIDE
    slots = length // LANES // 2
    owned = slots // devices
    runs = parted(owned)
    pieces = len(runs)
    field = convergence[0]
    table = jnp.asarray(column_table(length).reshape(devices, owned, 4 * LANES, 2 * LANES))
    tables = [jnp.asarray(t) for t in ray_tables(length // STRIDE, own * devices, length)]
    factors = jnp.asarray(field_factors(length).reshape(devices, owned, TILE, LANES))
    grouped, sums = over_groups(field)
    grouped = grouped.reshape(devices, owned, *grouped.shape[1:])
    totals = column_totals(sums)
    place = jnp.stack([lax.axis_index("row"), lax.axis_index("col") * owned]).astype(jnp.int32)

    def send(step, *after):
        begin, count = runs[step]
        held = lax.optimization_barrier((grouped, *after))[0]
        return over_lanes(held, table, begin, count)

    def exchange(value):
        return lax.all_to_all(value, "col", split_axis=0, concat_axis=0, tiled=True)

    sent = {step: send(step) for step in range(min(2, pieces))}
    arrived, partial, summed = {}, {}, {}
    for step, (begin, count) in enumerate(runs):
        arrived[step] = exchange(sent[step])
        if step + 2 < pieces:
            sent[step + 2] = send(step + 2, arrived[step])
        held = arrived[step]
        if step + 2 < pieces:
            held = lax.optimization_barrier((held, sent[step + 2]))[0]
        held = held.reshape(devices, count, STRIDE, own, 2 * LANES)
        shift = jnp.asarray(np.array([0, begin], np.int32))
        mean = None
        if begin == 0:
            late = lax.optimization_barrier((totals, arrived[step]))[0]
            mean = jnp.mean(late[0]).reshape(1)
        partial[step] = to_rays(place + shift, mean, held, tables, planes)
        summed[step] = lax.psum_scatter(
            partial[step], "row", scatter_dimension=0, tiled=True
        )[0]
    done = {}
    for step, (begin, _) in enumerate(runs):
        held = summed[step]
        if step == pieces - 1:
            held = lax.optimization_barrier((held, *done.values()))[0]
        done[begin] = back_over_lanes(exchange(held), table, factors, begin)
    parts = [done[begin] for begin in sorted(done)]
    base = curvature_sum(field, late)

    def run_local(start):
        return advance(lens_weight, parts, base, start)[None]

    shell_index = lax.axis_index("shell")
    outputs = run_local(rays_in)
    for group in range(1, lax.axis_size("shell")):
        received = passed_along(outputs[-1], "shell", 1)
        outputs = jnp.where(shell_index == group, run_local(received), outputs)
    return outputs


def solution(mesh):
    in_specs = (P("shell", ("row", "col"), None), P("shell"), P(None, ("row", "col"), None))
    out_specs = P("shell", None, ("row", "col"), None)
    return jax.shard_map(body, mesh=mesh, in_specs=in_specs, out_specs=out_specs, check_vma=False)
```
